32 devices in a mesh: mesh: 4 (over y, core), mode: 8 (over z, x).
Axes of the slice: x: 2, y: 2, z: 4, core: 2. Of those that a mesh axis runs over, the one named last changes fastest.
Arguments:
- field: float32 [256, 512, 1024], P('mode', 'mesh'), may hold values from -6 to 6
- kappa: bfloat16 [3, 512, 1024], P(None, ('mesh', 'mode')), may hold values from 0.099609375 to 1
- mass: float32 [512, 1024], P(('mesh', 'mode')), may hold values from 0.5 to 1.5
- kl_modes: bfloat16 [3, 256, 256], replicated, may hold values from -0.375 to 0.375
- to_points: bfloat16 [512, 256], replicated, may hold values from -0.375 to 0.375
- from_points: bfloat16 [256, 512], replicated, may hold values from -0.25 to 0.25
- capacity: float32 [512], replicated, may hold values from 0.5 to 2
- latent: float32 [512], replicated, may hold values from 0.5 to 3
Outputs:
- residual: bfloat16 [256, 512, 1024], P('mode', 'mesh')
The draws below stay inside these ranges and needn't reach their ends.
All inputs are finite; a program needn't handle non-finite values.
Results may differ from the reference program's by a relative error of at most 0.0058.
Values may be sent and summed in bfloat16 or wider, within the bound.
A program may use at most 256 MiB of HBM per device.

```python
import math
import jax
import jax.numpy as jnp
from jax import lax

P_SIZE = 256
Q = 512
KL = 3
NY = 1024
NX = 512


def block_scale(key, extent, cuts, low, largest):
    def one(axis_at, shards_of):
        draws = jax.random.uniform(jax.random.fold_in(jax.random.fold_in(key, 6), axis_at), (shards_of,), jnp.float32, low / len(cuts), largest / len(cuts))
        return jnp.repeat(jnp.exp(draws), extent[axis_at] // shards_of).reshape((-1,) + (1,) * (len(extent) - axis_at - 1))

    loudness = one(*cuts[0])
    for cut in cuts[1:]:
        loudness = loudness * one(*cut)
    return loudness


def normal_values(own_key, shape, deviation, most, pieces=(), held_as=jnp.bfloat16):
    loudness = block_scale(own_key, shape, pieces, -0.22, 0.18) if pieces else 1.0
    drawn = jax.random.normal(own_key, shape, jnp.float32) * deviation * loudness
    return jnp.minimum(jnp.maximum(drawn, -most), most).astype(held_as)


def setup_inputs(seed: int = 0) -> dict:
    streams_of = jax.random.split(jax.random.key(seed), 9)
    return {
        "field": normal_values(streams_of[0], (P_SIZE, NX, NY), 1.0, 6.0, ((0, 8), (1, 4)), jnp.float32),
        "kappa": jnp.clip(jnp.exp(math.log(1.0) - 2.306499 * jax.random.uniform(streams_of[1], (KL, NX, NY), jnp.float32) ** block_scale(streams_of[1], (KL, NX, NY), ((1, 32),), -0.2, 0.2)), 0.099609375, 1.0).astype(jnp.bfloat16),
        "mass": jnp.clip(1.0 + 0.1 * jax.random.normal(streams_of[2], (NX, NY), jnp.float32), 0.5, 1.5),
        "kl_modes": normal_values(streams_of[3], (KL, P_SIZE, P_SIZE), P_SIZE ** -0.5, 0.375),
        "to_points": normal_values(streams_of[4], (Q, P_SIZE), P_SIZE ** -0.5, 0.375),
        "from_points": normal_values(streams_of[5], (P_SIZE, Q), Q ** -0.5, 0.25),
        "capacity": jnp.clip(jnp.exp(jax.random.uniform(streams_of[6], (Q,), jnp.float32, math.log(0.5), math.log(2.0))), 0.5, 2.0),
        "latent": jnp.clip(jnp.exp(jax.random.uniform(streams_of[7], (Q,), jnp.float32, math.log(0.5), math.log(3.0))), 0.5, 3.0),
    }


def conduct(values, kappa):
    count = values.shape[1] - 2
    width = values.shape[2]
    vals = jnp.pad(values.astype(jnp.float32), ((0, 0), (0, 0), (1, 1)))[None]
    kaps = jnp.pad(kappa.astype(jnp.float32), ((0, 0), (0, 0), (1, 1)))[:, None]
    centre = vals[:, :, 1:1 + count, 1:1 + width]
    kcentre = kaps[:, :, 1:1 + count, 1:1 + width]
    total = jnp.zeros((kaps.shape[0], vals.shape[1], count, width), jnp.float32)
    for shift_x, shift_y in ((0, 1), (2, 1), (1, 0), (1, 2)):
        other = vals[:, :, shift_x:shift_x + count, shift_y:shift_y + width]
        kother = kaps[:, :, shift_x:shift_x + count, shift_y:shift_y + width]
        total = total + 0.5 * (kcentre + kother) * (centre - other)
    return total.astype(jnp.bfloat16)


def finish(coarse, images, mass_rows, kl_modes, to_points, from_points, capacity, latent):
    mixed = jnp.einsum('kij,kjxy->ixy', kl_modes.astype(jnp.float32), images.astype(jnp.float32))
    temps = jnp.einsum('qi,ixy->qxy', to_points.astype(jnp.float32), coarse.astype(jnp.float32))
    heat = (capacity[:, None, None] * temps + latent[:, None, None] * jax.nn.sigmoid(2.0 * temps)).astype(jnp.bfloat16)
    enthalpy = jnp.einsum('iq,qxy->ixy', from_points.astype(jnp.float32), heat.astype(jnp.float32))
    return (mass_rows[None] * enthalpy + mixed).astype(jnp.bfloat16)


def reference(field, kappa, mass, kl_modes, to_points, from_points, capacity, latent):
    coarse = field.astype(jnp.bfloat16)
    modes, rows_all, width = field.shape
    padded = jnp.pad(coarse, ((0, 0), (1, 1), (0, 0)))
    kpadded = jnp.pad(kappa, ((0, 0), (1, 1), (0, 0)))
    step_rows = 8

    def block(index):
        start = index * step_rows
        values = lax.dynamic_slice_in_dim(padded, start, step_rows + 2, 1)
        kaps = lax.dynamic_slice_in_dim(kpadded, start, step_rows + 2, 1)
        images = conduct(values, kaps)
        own = lax.dynamic_slice_in_dim(coarse, start, step_rows, 1)
        mass_rows = lax.dynamic_slice_in_dim(mass, start, step_rows, 0)
        return finish(own, images, mass_rows, kl_modes, to_points, from_points, capacity, latent)

    blocks = lax.map(block, jnp.arange(rows_all // step_rows, dtype=jnp.int32))
    return jnp.moveaxis(blocks, 0, 1).reshape(modes, rows_all, width)
```

```python
import functools

import jax
import jax.numpy as jnp
from jax import lax
from jax.experimental import pallas as pl
from jax.experimental.pallas import tpu as pltpu
from jax.sharding import PartitionSpec as P

STEP = 2
BAND = 16
TILE = 256


def halo(rows, axes):
    count = lax.axis_size(axes)
    up = lax.ppermute(rows[-1:], axes, [(i, i + 1) for i in range(count - 1)])
    down = lax.ppermute(rows[:1], axes, [(i + 1, i) for i in range(count - 1)])
    return up, down


def weights_of(kappa):
    rows = jnp.moveaxis(kappa, 1, 0)
    up, down = halo(rows, ("mesh", "mode"))
    ext = jnp.concatenate([up, rows, down], 0).astype(jnp.float32)
    count, terms, width = rows.shape
    ext = jnp.pad(ext, ((0, 0), (0, 0), (1, 1)))
    centre = ext[1:-1, :, 1:-1]
    others = (ext[:-2, :, 1:-1], ext[2:, :, 1:-1], ext[1:-1, :, :-2], ext[1:-1, :, 2:])
    return jnp.stack([0.5 * (centre + other) for other in others], 2).reshape(count, terms * 4, width)


def kernel(groups, src, coef, mass, kl, tp, fp, cap, lat, out, gath, res, img, recv_in, send_in, send_out, recv_out):
    me = lax.axis_index("mode")
    owned = src.shape[1]
    width = src.shape[2]
    nrows = res.shape[0]
    modes = res.shape[1]
    terms = coef.shape[1] // 4
    steps = nrows // STEP
    peers = [lax.rem(me + s, groups) for s in range(1, groups)]
    mine = pl.ds(pl.multiple_of(me * owned, owned), owned)
    others = pl.ds(0, modes - owned)

    barrier = pltpu.get_barrier_semaphore()
    for peer in peers:
        pl.semaphore_signal(barrier, inc=1, device_id={"mode": peer}, device_id_type=pl.DeviceIdType.MESH)
    pl.semaphore_wait(barrier, groups - 1)

    def send_chunk(c, carry):
        here = pl.ds(c * STEP, STEP)
        for peer in peers:
            pltpu.make_async_remote_copy(
                src_ref=src.at[pl.ds(peer * nrows + c * STEP, STEP)],
                dst_ref=gath.at[here, mine, :],
                send_sem=send_in,
                recv_sem=recv_in.at[c],
                device_id={"mode": peer},
                device_id_type=pl.DeviceIdType.MESH,
            ).start()
        pltpu.make_async_copy(
            src.at[pl.ds(me * nrows + c * STEP, STEP)], gath.at[here, mine, :], recv_in.at[c]
        ).start()
        return carry

    lax.fori_loop(0, steps + 1, send_chunk, 0)

    def wait_chunk(c):
        part = gath.at[pl.ds(c * STEP, STEP)]
        pltpu.make_async_copy(part, part, recv_in.at[c]).wait()

    wait_chunk(0)
    cols = lax.broadcasted_iota(jnp.int32, (BAND, width), 1)
    first = cols == 0
    last = cols == width - 1

    def row(r):
        @pl.loop(0, modes // BAND)
        def _(b):
            band = pl.ds(pl.multiple_of(b * BAND, BAND), BAND)
            v = gath[r + 1, band, :].astype(jnp.float32)
            diffs = (
                v - gath[r, band, :].astype(jnp.float32),
                v - gath[r + 2, band, :].astype(jnp.float32),
                v - jnp.where(first, 0.0, pltpu.roll(v, 1, 1)),
                v - jnp.where(last, 0.0, pltpu.roll(v, width - 1, 1)),
            )
            for k in range(terms):
                total = coef[r, 4 * k : 4 * k + 1, :] * diffs[0]
                for d in range(1, 4):
                    total = total + coef[r, 4 * k + d : 4 * k + d + 1, :] * diffs[d]
                img[pl.ds(pl.multiple_of(k * modes + b * BAND, BAND), BAND), :] = total.astype(jnp.bfloat16)

        @pl.loop(0, width // TILE)
        def _(t):
            tile = pl.ds(pl.multiple_of(t * TILE, TILE), TILE)
            temps = jnp.dot(tp[...], gath[r + 1, :, tile], preferred_element_type=jnp.float32)
            half = lat[...] * 0.5
            heat = (cap[...] * temps + (half + half * jnp.tanh(temps))).astype(jnp.bfloat16)
            enthalpy = jnp.dot(fp[...], heat, preferred_element_type=jnp.float32)
            mixed = jnp.dot(kl[...], img[:, tile], preferred_element_type=jnp.float32)
            res[r, :, tile] = (mass[r, :, tile] * enthalpy + mixed).astype(jnp.bfloat16)

    def step(p, carry):
        wait_chunk(p + 1)

        @pl.loop(0, STEP)
        def _(i):
            row(p * STEP + i)

        here = pl.ds(p * STEP, STEP)
        there = out.at[pl.ds(me * nrows + p * STEP, STEP)]
        for peer in peers:
            pltpu.make_async_remote_copy(
                src_ref=res.at[here, pl.ds(pl.multiple_of(peer * owned, owned), owned), :],
                dst_ref=there,
                send_sem=send_out,
                recv_sem=recv_out,
                device_id={"mode": peer},
                device_id_type=pl.DeviceIdType.MESH,
            ).start()
        pltpu.make_async_copy(res.at[here, mine, :], there, recv_out).start()
        return carry

    lax.fori_loop(0, steps, step, 0)

    sent = gath.at[:, others, :]
    pltpu.make_async_copy(sent, sent, send_in).wait()
    sent = res.at[:, others, :]
    pltpu.make_async_copy(sent, sent, send_out).wait()
    pltpu.make_async_copy(out, out, recv_out).wait()


def exchange(ext, coef, mass, kl, tp, fp, cap, lat):
    groups = lax.axis_size("mode")
    owned, width = ext.shape[1:]
    nrows, modes = mass.shape[0], tp.shape[1]
    vmem = pl.BlockSpec(memory_space=pltpu.VMEM)
    hbm = pl.BlockSpec(memory_space=pl.ANY)
    work = modes * nrows * width
    return pl.pallas_call(
        functools.partial(kernel, groups),
        out_shape=jax.ShapeDtypeStruct((nrows * groups, owned, width), jnp.bfloat16),
        in_specs=[hbm] + [vmem] * 7,
        out_specs=hbm,
        scratch_shapes=[
            pltpu.VMEM((nrows + STEP, modes, width), jnp.bfloat16),
            pltpu.VMEM((nrows, modes, width), jnp.bfloat16),
            pltpu.VMEM((kl.shape[1], width), jnp.bfloat16),
            pltpu.SemaphoreType.DMA((nrows // STEP + 1,)),
            pltpu.SemaphoreType.DMA,
            pltpu.SemaphoreType.DMA,
            pltpu.SemaphoreType.DMA,
        ],
        compiler_params=pltpu.CompilerParams(
            collective_id=0, has_side_effects=True, vmem_limit_bytes=44 * 1024 * 1024
        ),
        cost_estimate=pl.CostEstimate(
            flops=2 * work * (kl.shape[1] + 2 * tp.shape[0]),
            bytes_accessed=4 * work,
            transcendentals=nrows * width * tp.shape[0],
        ),
    )(ext, coef, mass[:, None, :], kl, tp, fp, cap[:, None], lat[:, None])


def exchange_small(ext, coef, mass, kl, tp, fp, cap, lat):
    groups = lax.axis_size("mode")
    owned, width = ext.shape[1:]
    nrows, modes = mass.shape[0], tp.shape[1]
    terms = coef.shape[1] // 4
    parts = jnp.stack([ext[d * nrows : d * nrows + nrows + 2] for d in range(groups)], 0)
    moved = lax.all_to_all(parts, "mode", split_axis=0, concat_axis=0, tiled=True)
    rows = jnp.moveaxis(moved, 0, 1).reshape(nrows + 2, modes, width)
    own = rows[1:-1]
    v = jnp.pad(rows.astype(jnp.float32), ((0, 0), (0, 0), (1, 1)))
    centre = v[1:-1, :, 1:-1]
    others = (v[:-2, :, 1:-1], v[2:, :, 1:-1], v[1:-1, :, :-2], v[1:-1, :, 2:])
    images = [
        sum(coef[:, 4 * k + d, None, :] * (centre - others[d]) for d in range(4)).astype(jnp.bfloat16)
        for k in range(terms)
    ]
    images = jnp.concatenate(images, 1)
    mixed = jnp.einsum("ij,rjx->rix", kl, images, preferred_element_type=jnp.float32)
    temps = jnp.einsum("qi,rix->rqx", tp, own, preferred_element_type=jnp.float32)
    heat = (cap[:, None] * temps + lat[:, None] * jax.nn.sigmoid(2.0 * temps)).astype(jnp.bfloat16)
    enthalpy = jnp.einsum("iq,rqx->rix", fp, heat, preferred_element_type=jnp.float32)
    result = (mass[:, None, :] * enthalpy + mixed).astype(jnp.bfloat16)
    result = result.reshape(nrows, groups, owned, width)
    back = lax.all_to_all(result, "mode", split_axis=1, concat_axis=0, tiled=True)
    return back.reshape(nrows * groups, owned, width)


def body(field, kappa, mass, kl_modes, to_points, from_points, capacity, latent):
    coarse = jnp.transpose(field.astype(jnp.bfloat16), (1, 0, 2))
    up, down = halo(coarse, "mesh")
    ext = jnp.concatenate([up, coarse, down], 0)
    coef = weights_of(kappa)
    terms, modes = kl_modes.shape[:2]
    kl = jnp.transpose(kl_modes, (1, 0, 2)).reshape(modes, terms * modes)
    nrows, owned = mass.shape[0], field.shape[0]
    fits = owned % 16 == 0 and nrows % STEP == 0 and field.shape[2] % TILE == 0
    run = exchange if fits else exchange_small
    out = run(ext, coef, mass, kl, to_points, from_points, capacity, latent)
    return jnp.transpose(out, (1, 0, 2))


def solution(mesh):
    in_specs = (
        P("mode", "mesh", None),
        P(None, ("mesh", "mode"), None),
        P(("mesh", "mode"), None),
        P(),
        P(),
        P(),
        P(),
        P(),
    )
    out_specs = P("mode", "mesh", None)
    return jax.shard_map(body, mesh=mesh, in_specs=in_specs, out_specs=out_specs, check_vma=False)
```

```python
import functools

import jax
import jax.numpy as jnp
from jax import lax
from jax.experimental import pallas as pl
from jax.experimental.pallas import tpu as pltpu
from jax.sharding import PartitionSpec as P

LOAD = 8
BAND = 16
TILE = 256


def halo(rows, axes):
    count = lax.axis_size(axes)
    up = lax.ppermute(rows[-1:], axes, [(i, i + 1) for i in range(count - 1)])
    down = lax.ppermute(rows[:1], axes, [(i + 1, i) for i in range(count - 1)])
    return up, down


def weights_of(kappa):
    rows = jnp.moveaxis(kappa, 1, 0)
    up, down = halo(rows, ("mesh", "mode"))
    ext = jnp.concatenate([up, rows, down], 0).astype(jnp.float32)
    count, terms, width = rows.shape
    ext = jnp.pad(ext, ((0, 0), (0, 0), (1, 1)))
    centre = ext[1:-1, :, 1:-1]
    others = (ext[:-2, :, 1:-1], ext[2:, :, 1:-1], ext[1:-1, :, :-2], ext[1:-1, :, 2:])
    return jnp.stack([0.5 * (centre + other) for other in others], 2).reshape(count, terms * 4, width)


def kernel(
    groups, parts, field, kap, mass, kl, tp, fp, cap, lat, out,
    buf, stage, gath, res, img, coef, kext,
    load, recv_rows, recv_halo, recv_kap, recv_out, send_in, send_edge, send_fwd, send_kap, send_out,
):
    me = lax.axis_index("mode")
    part = lax.axis_index("mesh")
    owned = field.shape[0]
    width = field.shape[2]
    nrows, modes = res.shape[:2]
    total_rows = nrows * groups
    terms = kap.shape[0]
    blocks = nrows // LOAD
    middle = groups // 2
    mine = pl.ds(pl.multiple_of(me * owned, owned), owned)
    others = pl.ds(0, modes - owned)
    peers = [lax.rem(me + s, groups) for s in range(1, groups)]
    has_prev = part > 0
    has_next = part < parts - 1
    opens = jnp.logical_or(me > 0, has_prev)
    closes = jnp.logical_or(me < groups - 1, has_next)

    def remote(src, dst, send, recv, device):
        return pltpu.make_async_remote_copy(
            src_ref=src, dst_ref=dst, send_sem=send, recv_sem=recv,
            device_id=device, device_id_type=pl.DeviceIdType.MESH,
        )

    def arrived(ref, sem):
        pltpu.make_async_copy(ref, ref, sem).wait()

    def block_load(i):
        peer = lax.rem(me + middle + i, groups)
        start = pl.multiple_of(peer * nrows + lax.div(i, groups) * LOAD, LOAD)
        slot = lax.rem(i, 2)
        return pltpu.make_async_copy(field.at[:, pl.ds(start, LOAD), :], buf.at[slot], load.at[slot])

    block_load(0).start()

    barrier = pltpu.get_barrier_semaphore()

    def greet(device):
        pl.semaphore_signal(barrier, inc=1, device_id=device, device_id_type=pl.DeviceIdType.MESH)

    for peer in peers:
        greet({"mode": peer})

    @pl.when(jnp.logical_and(me == 0, has_prev))
    def _():
        for j in range(groups):
            greet({"mesh": part - 1, "mode": j})

    @pl.when(jnp.logical_and(me == groups - 1, has_next))
    def _():
        for j in range(groups):
            greet({"mesh": part + 1, "mode": j})

    pl.semaphore_wait(barrier, groups - 1 + has_prev.astype(jnp.int32) + has_next.astype(jnp.int32))

    before = {
        "mesh": jnp.where(me == 0, part - 1, part),
        "mode": lax.rem(me + groups - 1, groups),
    }
    after = {
        "mesh": jnp.where(me == groups - 1, part + 1, part),
        "mode": lax.rem(me + 1, groups),
    }
    kap_after = remote(kap, kext.at[0], send_kap.at[0], recv_kap.at[0], after)
    kap_before = remote(kap, kext.at[1], send_kap.at[1], recv_kap.at[1], before)

    @pl.when(closes)
    def _():
        kap_after.start()

    @pl.when(opens)
    def _():
        kap_before.start()

    def send_block(i, carry):
        block_load(i).wait()

        @pl.when(i + 1 < blocks * groups)
        def _():
            block_load(i + 1).start()

        peer = lax.rem(me + middle + i, groups)
        h = lax.div(i, groups)
        start = peer * nrows + h * LOAD
        slot = lax.rem(i, 2)
        for q in range(0, owned, 16):
            stage[pl.ds(start, LOAD), q : q + 16, :] = jnp.swapaxes(buf[slot, q : q + 16], 0, 1).astype(stage.dtype)
        rows = stage.at[pl.ds(start, LOAD)]
        there = gath.at[pl.ds(1 + h * LOAD, LOAD), mine, :]

        @pl.when(peer != me)
        def _():
            remote(rows, there, send_in, recv_rows.at[h], {"mode": peer}).start()

        @pl.when(peer == me)
        def _():
            pltpu.make_async_copy(rows, there, recv_rows.at[h]).start()

        return carry

    lax.fori_loop(0, blocks * groups, send_block, 0)

    top = gath.at[pl.ds(0, 1)]
    bottom = gath.at[pl.ds(nrows + 1, 1)]
    my_top = gath.at[pl.ds(0, 1), mine, :]
    my_bottom = gath.at[pl.ds(nrows + 1, 1), mine, :]
    centre = middle * nrows
    above = stage.at[pl.ds(centre - 1, 1)]
    below = stage.at[pl.ds(centre, 1)]
    edges = [
        (me != middle, remote(above, my_top, send_edge.at[0], recv_halo.at[0], {"mode": middle})),
        (me != middle - 1, remote(below, my_bottom, send_edge.at[1], recv_halo.at[1], {"mode": middle - 1})),
        (
            has_next,
            remote(
                stage.at[pl.ds(total_rows - 1, 1)], my_top, send_edge.at[2], recv_halo.at[0],
                {"mesh": part + 1, "mode": 0},
            ),
        ),
        (
            has_prev,
            remote(
                stage.at[pl.ds(0, 1)], my_bottom, send_edge.at[3], recv_halo.at[1],
                {"mesh": part - 1, "mode": groups - 1},
            ),
        ),
    ]
    for wanted, copy in edges:
        pl.when(wanted)(copy.start)

    @pl.when(me == middle)
    def _():
        pltpu.make_async_copy(above, my_top, recv_halo.at[0]).start()

    @pl.when(me == middle - 1)
    def _():
        pltpu.make_async_copy(below, my_bottom, recv_halo.at[1]).start()

    @pl.when(jnp.logical_not(opens))
    def _():
        gath[0] = jnp.zeros((modes, width), gath.dtype)
        kext[0] = jnp.zeros(kap.shape, kap.dtype)

    @pl.when(jnp.logical_not(closes))
    def _():
        gath[nrows + 1] = jnp.zeros((modes, width), gath.dtype)
        kext[1] = jnp.zeros(kap.shape, kap.dtype)

    @pl.when(opens)
    def _():
        arrived(kext.at[0], recv_kap.at[0])

    @pl.when(closes)
    def _():
        arrived(kext.at[1], recv_kap.at[1])

    at_row = lax.broadcasted_iota(jnp.int32, (nrows, width), 0)
    at_col = lax.broadcasted_iota(jnp.int32, (nrows, width), 1)
    for k in range(terms):
        c = kap[k].astype(jnp.float32)
        up = kext[0, k].astype(jnp.float32)[nrows - 1 :, :]
        down = kext[1, k].astype(jnp.float32)[:1, :]
        near = (
            jnp.where(at_row == 0, up, pltpu.roll(c, 1, 0)),
            jnp.where(at_row == nrows - 1, down, pltpu.roll(c, nrows - 1, 0)),
            jnp.where(at_col == 0, 0.0, pltpu.roll(c, 1, 1)),
            jnp.where(at_col == width - 1, 0.0, pltpu.roll(c, width - 1, 1)),
        )
        for d in range(4):
            coef[4 * k + d] = 0.5 * (c + near[d])

    cols = lax.broadcasted_iota(jnp.int32, (BAND, width), 1)
    first = cols == 0
    last = cols == width - 1

    def row(r):
        here = pl.ds(r, 1)

        @pl.loop(0, modes // BAND)
        def _(b):
            band = pl.ds(pl.multiple_of(b * BAND, BAND), BAND)
            v = gath[r + 1, band, :].astype(jnp.float32)
            diffs = (
                v - gath[r, band, :].astype(jnp.float32),
                v - gath[r + 2, band, :].astype(jnp.float32),
                v - jnp.where(first, 0.0, pltpu.roll(v, 1, 1)),
                v - jnp.where(last, 0.0, pltpu.roll(v, width - 1, 1)),
            )
            for k in range(terms):
                total = coef[4 * k, here, :] * diffs[0]
                for d in range(1, 4):
                    total = total + coef[4 * k + d, here, :] * diffs[d]
                img[k, band, :] = total.astype(jnp.bfloat16)

        @pl.loop(0, width // TILE)
        def _(t):
            tile = pl.ds(pl.multiple_of(t * TILE, TILE), TILE)
            temps = jnp.dot(tp[...], gath[r + 1, :, tile], preferred_element_type=jnp.float32)
            half = lat[...] * 0.5
            heat = (cap[...] * temps + (half + half * jnp.tanh(temps))).astype(jnp.bfloat16)
            enthalpy = jnp.dot(fp[...], heat, preferred_element_type=jnp.float32)
            mixed = jnp.dot(kl[0], img[0, :, tile], preferred_element_type=jnp.float32)
            for k in range(1, terms):
                mixed = mixed + jnp.dot(kl[k], img[k, :, tile], preferred_element_type=jnp.float32)
            res[r, :, tile] = (mass[here, tile] * enthalpy + mixed).astype(jnp.bfloat16)

    gives_after = jnp.logical_and(me != middle - 1, me != groups - 1)
    gives_before = jnp.logical_and(me != middle, me != 0)
    fwd_after = remote(
        gath.at[pl.ds(nrows, 1)], top, send_fwd.at[0], recv_halo.at[0], {"mode": lax.rem(me + 1, groups)}
    )
    fwd_before = remote(
        gath.at[pl.ds(1, 1)], bottom, send_fwd.at[1], recv_halo.at[1], {"mode": lax.rem(me + groups - 1, groups)}
    )

    arrived(gath.at[pl.ds(1, LOAD)], recv_rows.at[0])
    pl.when(gives_before)(fwd_before.start)

    def step(t, carry):
        @pl.when(jnp.logical_and(lax.rem(t + 2, LOAD) == 0, t < nrows - 2))
        def _():
            h = lax.div(t + 2, LOAD)
            arrived(gath.at[pl.ds(1 + h * LOAD, LOAD)], recv_rows.at[h])

        @pl.when(jnp.logical_and(t == (blocks - 1) * LOAD - 2, gives_after))
        def _():
            fwd_after.start()

        @pl.when(jnp.logical_and(t == nrows - 2, opens))
        def _():
            arrived(top, recv_halo.at[0])

        @pl.when(jnp.logical_and(t == nrows - 1, closes))
        def _():
            arrived(bottom, recv_halo.at[1])

        r = jnp.where(t < nrows - 2, t + 1, (t - (nrows - 2)) * (nrows - 1))
        row(r)
        here = pl.ds(r, 1)
        there = out.at[pl.ds(me * nrows + r, 1)]
        for peer in [peers[(s + middle - 1) % (groups - 1)] for s in range(groups - 1)]:
            part_of = res.at[here, pl.ds(pl.multiple_of(peer * owned, owned), owned), :]
            remote(part_of, there, send_out, recv_out, {"mode": peer}).start()
        pltpu.make_async_copy(res.at[here, mine, :], there, recv_out).start()
        return carry

    lax.fori_loop(0, nrows, step, 0)

    pl.when(closes)(kap_after.wait_send)
    pl.when(opens)(kap_before.wait_send)
    for wanted, copy in edges:
        pl.when(wanted)(copy.wait_send)
    pl.when(gives_after)(fwd_after.wait_send)
    pl.when(gives_before)(fwd_before.wait_send)
    arrived(gath.at[pl.ds(0, nrows), others, :], send_in)
    arrived(res.at[:, others, :], send_out)
    arrived(out, recv_out)


def exchange(field, kappa, mass, kl, tp, fp, cap, lat):
    groups, parts = lax.axis_size("mode"), lax.axis_size("mesh")
    owned, total_rows, width = field.shape
    nrows, modes = mass.shape[0], tp.shape[1]
    terms = kl.shape[0]
    vmem = pl.BlockSpec(memory_space=pltpu.VMEM)
    hbm = pl.BlockSpec(memory_space=pl.ANY)
    work = modes * nrows * width
    dma = pltpu.SemaphoreType.DMA
    return pl.pallas_call(
        functools.partial(kernel, groups, parts),
        out_shape=jax.ShapeDtypeStruct((total_rows, owned, width), jnp.bfloat16),
        in_specs=[hbm] + [vmem] * 7,
        out_specs=hbm,
        scratch_shapes=[
            pltpu.VMEM((2, owned, LOAD, width), jnp.float32),
            pltpu.VMEM((total_rows, owned, width), jnp.bfloat16),
            pltpu.VMEM((nrows + 2, modes, width), jnp.bfloat16),
            pltpu.VMEM((nrows, modes, width), jnp.bfloat16),
            pltpu.VMEM((terms, modes, width), jnp.bfloat16),
            pltpu.VMEM((terms * 4, nrows, width), jnp.float32),
            pltpu.VMEM((2,) + kappa.shape, jnp.bfloat16),
            dma((2,)),
            dma((nrows // LOAD,)),
            dma((2,)),
            dma((2,)),
            dma,
            dma,
            dma((4,)),
            dma((2,)),
            dma((2,)),
            dma,
        ],
        compiler_params=pltpu.CompilerParams(
            collective_id=0, has_side_effects=True, vmem_limit_bytes=48 * 1024 * 1024
        ),
        cost_estimate=pl.CostEstimate(
            flops=2 * work * (terms * modes + 2 * tp.shape[0]),
            bytes_accessed=6 * work,
            transcendentals=nrows * width * tp.shape[0],
        ),
    )(field, kappa, mass, kl, tp, fp, cap[:, None], lat[:, None])


def exchange_small(ext, coef, mass, kl, tp, fp, cap, lat):
    groups = lax.axis_size("mode")
    owned, width = ext.shape[1:]
    nrows, modes = mass.shape[0], tp.shape[1]
    terms = coef.shape[1] // 4
    parts = jnp.stack([ext[d * nrows : d * nrows + nrows + 2] for d in range(groups)], 0)
    moved = lax.all_to_all(parts, "mode", split_axis=0, concat_axis=0, tiled=True)
    rows = jnp.moveaxis(moved, 0, 1).reshape(nrows + 2, modes, width)
    own = rows[1:-1]
    v = jnp.pad(rows.astype(jnp.float32), ((0, 0), (0, 0), (1, 1)))
    centre = v[1:-1, :, 1:-1]
    others = (v[:-2, :, 1:-1], v[2:, :, 1:-1], v[1:-1, :, :-2], v[1:-1, :, 2:])
    images = [
        sum(coef[:, 4 * k + d, None, :] * (centre - others[d]) for d in range(4)).astype(jnp.bfloat16)
        for k in range(terms)
    ]
    images = jnp.concatenate(images, 1)
    mixed = jnp.einsum("ij,rjx->rix", kl, images, preferred_element_type=jnp.float32)
    temps = jnp.einsum("qi,rix->rqx", tp, own, preferred_element_type=jnp.float32)
    heat = (cap[:, None] * temps + lat[:, None] * jax.nn.sigmoid(2.0 * temps)).astype(jnp.bfloat16)
    enthalpy = jnp.einsum("iq,rqx->rix", fp, heat, preferred_element_type=jnp.float32)
    result = (mass[:, None, :] * enthalpy + mixed).astype(jnp.bfloat16)
    result = result.reshape(nrows, groups, owned, width)
    back = lax.all_to_all(result, "mode", split_axis=1, concat_axis=0, tiled=True)
    return back.reshape(nrows * groups, owned, width)


def body(field, kappa, mass, kl_modes, to_points, from_points, capacity, latent):
    nrows, owned = mass.shape[0], field.shape[0]
    fits = owned % 16 == 0 and nrows % 16 == 0 and field.shape[2] % TILE == 0
    if fits:
        out = exchange(field, kappa, mass, kl_modes, to_points, from_points, capacity, latent)
        return jnp.transpose(out, (1, 0, 2))
    coarse = jnp.transpose(field.astype(jnp.bfloat16), (1, 0, 2))
    up, down = halo(coarse, "mesh")
    ext = jnp.concatenate([up, coarse, down], 0)
    coef = weights_of(kappa)
    terms, modes = kl_modes.shape[:2]
    kl = jnp.transpose(kl_modes, (1, 0, 2)).reshape(modes, terms * modes)
    out = exchange_small(ext, coef, mass, kl, to_points, from_points, capacity, latent)
    return jnp.transpose(out, (1, 0, 2))


def solution(mesh):
    in_specs = (
        P("mode", "mesh", None),
        P(None, ("mesh", "mode"), None),
        P(("mesh", "mode"), None),
        P(),
        P(),
        P(),
        P(),
        P(),
    )
    out_specs = P("mode", "mesh", None)
    return jax.shard_map(body, mesh=mesh, in_specs=in_specs, out_specs=out_specs, check_vma=False)
```

```python
import functools

import jax
import jax.numpy as jnp
from jax import lax
from jax.experimental import pallas as pl
from jax.experimental.pallas import tpu as pltpu
from jax.sharding import PartitionSpec as P

LOAD = 8
BAND = 16
TILE = 256


def halo(rows, axes):
    count = lax.axis_size(axes)
    up = lax.ppermute(rows[-1:], axes, [(i, i + 1) for i in range(count - 1)])
    down = lax.ppermute(rows[:1], axes, [(i + 1, i) for i in range(count - 1)])
    return up, down


def weights_of(kappa):
    rows = jnp.moveaxis(kappa, 1, 0)
    up, down = halo(rows, ("mesh", "mode"))
    ext = jnp.concatenate([up, rows, down], 0).astype(jnp.float32)
    count, terms, width = rows.shape
    ext = jnp.pad(ext, ((0, 0), (0, 0), (1, 1)))
    centre = ext[1:-1, :, 1:-1]
    others = (ext[:-2, :, 1:-1], ext[2:, :, 1:-1], ext[1:-1, :, :-2], ext[1:-1, :, 2:])
    return jnp.stack([0.5 * (centre + other) for other in others], 2).reshape(count, terms * 4, width)


def kernel(
    groups, parts, field, kap, mass, kl_all, tp_all, fp_all, cap, lat, out,
    buf, stage, gath, res, img, coef, kext, kl, tp, fp,
    load, recv_rows, recv_halo, recv_kap, recv_out, send_in, send_edge, send_fwd, send_kap, send_out, fetch,
):
    me = lax.axis_index("mode")
    part = lax.axis_index("mesh")
    owned = field.shape[0]
    width = field.shape[2]
    nrows, modes = res.shape[:2]
    total_rows = nrows * groups
    terms = kap.shape[0]
    blocks = nrows // LOAD
    middle = groups // 2
    mine = pl.ds(pl.multiple_of(me * owned, owned), owned)
    others = pl.ds(0, modes - owned)
    peers = [lax.rem(me + s, groups) for s in range(1, groups)]
    has_prev = part > 0
    has_next = part < parts - 1
    opens = jnp.logical_or(me > 0, has_prev)
    closes = jnp.logical_or(me < groups - 1, has_next)

    def remote(src, dst, send, recv, device):
        return pltpu.make_async_remote_copy(
            src_ref=src, dst_ref=dst, send_sem=send, recv_sem=recv,
            device_id=device, device_id_type=pl.DeviceIdType.MESH,
        )

    def arrived(ref, sem):
        pltpu.make_async_copy(ref, ref, sem).wait()

    way = 1 - 2 * lax.rem(part, 2)

    def partner(i):
        return lax.rem(me + middle + groups + way * lax.rem(i, groups), groups)

    def block_load(i):
        peer = partner(i)
        start = pl.multiple_of(peer * nrows + lax.div(i, groups) * LOAD, LOAD)
        slot = lax.rem(i, 2)
        return pltpu.make_async_copy(field.at[:, pl.ds(start, LOAD), :], buf.at[slot], load.at[slot])

    block_load(0).start()
    fetches = [
        pltpu.make_async_copy(whole, held, fetch.at[n])
        for n, (whole, held) in enumerate(((kl_all, kl), (tp_all, tp), (fp_all, fp)))
    ]
    for copy in fetches:
        copy.start()

    barrier = pltpu.get_barrier_semaphore()

    def greet(device):
        pl.semaphore_signal(barrier, inc=1, device_id=device, device_id_type=pl.DeviceIdType.MESH)

    for peer in peers:
        greet({"mode": peer})

    @pl.when(jnp.logical_and(me == 0, has_prev))
    def _():
        for j in range(groups):
            greet({"mesh": part - 1, "mode": j})

    @pl.when(jnp.logical_and(me == groups - 1, has_next))
    def _():
        for j in range(groups):
            greet({"mesh": part + 1, "mode": j})

    pl.semaphore_wait(barrier, groups - 1 + has_prev.astype(jnp.int32) + has_next.astype(jnp.int32))

    before = {
        "mesh": jnp.where(me == 0, part - 1, part),
        "mode": lax.rem(me + groups - 1, groups),
    }
    after = {
        "mesh": jnp.where(me == groups - 1, part + 1, part),
        "mode": lax.rem(me + 1, groups),
    }
    kap_after = remote(kap, kext.at[0], send_kap.at[0], recv_kap.at[0], after)
    kap_before = remote(kap, kext.at[1], send_kap.at[1], recv_kap.at[1], before)

    @pl.when(closes)
    def _():
        kap_after.start()

    @pl.when(opens)
    def _():
        kap_before.start()

    def send_block(i, carry):
        block_load(i).wait()

        @pl.when(i + 1 < blocks * groups)
        def _():
            block_load(i + 1).start()

        peer = partner(i)
        h = lax.div(i, groups)
        start = peer * nrows + h * LOAD
        slot = lax.rem(i, 2)
        for q in range(0, owned, 16):
            stage[pl.ds(start, LOAD), q : q + 16, :] = jnp.swapaxes(buf[slot, q : q + 16], 0, 1).astype(stage.dtype)
        rows = stage.at[pl.ds(start, LOAD)]
        there = gath.at[pl.ds(1 + h * LOAD, LOAD), mine, :]

        @pl.when(peer != me)
        def _():
            remote(rows, there, send_in, recv_rows.at[h], {"mode": peer}).start()

        @pl.when(peer == me)
        def _():
            pltpu.make_async_copy(rows, there, recv_rows.at[h]).start()

        return carry

    lax.fori_loop(0, blocks * groups, send_block, 0)

    top = gath.at[pl.ds(0, 1)]
    bottom = gath.at[pl.ds(nrows + 1, 1)]
    my_top = gath.at[pl.ds(0, 1), mine, :]
    my_bottom = gath.at[pl.ds(nrows + 1, 1), mine, :]
    centre = middle * nrows
    above = stage.at[pl.ds(centre - 1, 1)]
    below = stage.at[pl.ds(centre, 1)]
    edges = [
        (me != middle, remote(above, my_top, send_edge.at[0], recv_halo.at[0], {"mode": middle})),
        (me != middle - 1, remote(below, my_bottom, send_edge.at[1], recv_halo.at[1], {"mode": middle - 1})),
        (
            has_next,
            remote(
                stage.at[pl.ds(total_rows - 1, 1)], my_top, send_edge.at[2], recv_halo.at[0],
                {"mesh": part + 1, "mode": 0},
            ),
        ),
        (
            has_prev,
            remote(
                stage.at[pl.ds(0, 1)], my_bottom, send_edge.at[3], recv_halo.at[1],
                {"mesh": part - 1, "mode": groups - 1},
            ),
        ),
    ]
    for wanted, copy in edges:
        pl.when(wanted)(copy.start)

    @pl.when(me == middle)
    def _():
        pltpu.make_async_copy(above, my_top, recv_halo.at[0]).start()

    @pl.when(me == middle - 1)
    def _():
        pltpu.make_async_copy(below, my_bottom, recv_halo.at[1]).start()

    @pl.when(jnp.logical_not(opens))
    def _():
        gath[0] = jnp.zeros((modes, width), gath.dtype)
        kext[0] = jnp.zeros(kap.shape, kap.dtype)

    @pl.when(jnp.logical_not(closes))
    def _():
        gath[nrows + 1] = jnp.zeros((modes, width), gath.dtype)
        kext[1] = jnp.zeros(kap.shape, kap.dtype)

    @pl.when(opens)
    def _():
        arrived(kext.at[0], recv_kap.at[0])

    @pl.when(closes)
    def _():
        arrived(kext.at[1], recv_kap.at[1])

    at_row = lax.broadcasted_iota(jnp.int32, (nrows, width), 0)
    at_col = lax.broadcasted_iota(jnp.int32, (nrows, width), 1)
    for k in range(terms):
        c = kap[k].astype(jnp.float32)
        up = kext[0, k].astype(jnp.float32)[nrows - 1 :, :]
        down = kext[1, k].astype(jnp.float32)[:1, :]
        near = (
            jnp.where(at_row == 0, up, pltpu.roll(c, 1, 0)),
            jnp.where(at_row == nrows - 1, down, pltpu.roll(c, nrows - 1, 0)),
            jnp.where(at_col == 0, 0.0, pltpu.roll(c, 1, 1)),
            jnp.where(at_col == width - 1, 0.0, pltpu.roll(c, width - 1, 1)),
        )
        for d in range(4):
            coef[4 * k + d] = 0.5 * (c + near[d])

    cols = lax.broadcasted_iota(jnp.int32, (BAND, width), 1)
    first = cols == 0
    last = cols == width - 1

    def row(r):
        here = pl.ds(r, 1)

        @pl.loop(0, modes // BAND)
        def _(b):
            band = pl.ds(pl.multiple_of(b * BAND, BAND), BAND)
            v = gath[r + 1, band, :].astype(jnp.float32)
            diffs = (
                v - gath[r, band, :].astype(jnp.float32),
                v - gath[r + 2, band, :].astype(jnp.float32),
                v - jnp.where(first, 0.0, pltpu.roll(v, 1, 1)),
                v - jnp.where(last, 0.0, pltpu.roll(v, width - 1, 1)),
            )
            for k in range(terms):
                total = coef[4 * k, here, :] * diffs[0]
                for d in range(1, 4):
                    total = total + coef[4 * k + d, here, :] * diffs[d]
                img[k, band, :] = total.astype(jnp.bfloat16)

        @pl.loop(0, width // TILE)
        def _(t):
            tile = pl.ds(pl.multiple_of(t * TILE, TILE), TILE)
            temps = jnp.dot(tp[...], gath[r + 1, :, tile], preferred_element_type=jnp.float32)
            half = lat[...] * 0.5
            heat = (cap[...] * temps + (half + half * jnp.tanh(temps))).astype(jnp.bfloat16)
            enthalpy = jnp.dot(fp[...], heat, preferred_element_type=jnp.float32)
            mixed = jnp.dot(kl[0], img[0, :, tile], preferred_element_type=jnp.float32)
            for k in range(1, terms):
                mixed = mixed + jnp.dot(kl[k], img[k, :, tile], preferred_element_type=jnp.float32)
            res[r, :, tile] = (mass[here, tile] * enthalpy + mixed).astype(jnp.bfloat16)

    gives_after = jnp.logical_and(me != middle - 1, me != groups - 1)
    gives_before = jnp.logical_and(me != middle, me != 0)
    fwd_after = remote(
        gath.at[pl.ds(nrows, 1)], top, send_fwd.at[0], recv_halo.at[0], {"mode": lax.rem(me + 1, groups)}
    )
    fwd_before = remote(
        gath.at[pl.ds(1, 1)], bottom, send_fwd.at[1], recv_halo.at[1], {"mode": lax.rem(me + groups - 1, groups)}
    )

    for copy in fetches:
        copy.wait()
    arrived(gath.at[pl.ds(1, LOAD)], recv_rows.at[0])
    pl.when(gives_before)(fwd_before.start)

    def step(t, carry):
        @pl.when(jnp.logical_and(lax.rem(t + 2, LOAD) == 0, t < nrows - 2))
        def _():
            h = lax.div(t + 2, LOAD)
            arrived(gath.at[pl.ds(1 + h * LOAD, LOAD)], recv_rows.at[h])

        @pl.when(jnp.logical_and(t == (blocks - 1) * LOAD - 2, gives_after))
        def _():
            fwd_after.start()

        @pl.when(jnp.logical_and(t == nrows - 2, opens))
        def _():
            arrived(top, recv_halo.at[0])

        @pl.when(jnp.logical_and(t == nrows - 1, closes))
        def _():
            arrived(bottom, recv_halo.at[1])

        r = jnp.where(t < nrows - 2, t + 1, (t - (nrows - 2)) * (nrows - 1))
        row(r)
        here = pl.ds(r, 1)
        there = out.at[pl.ds(me * nrows + r, 1)]
        for peer in [partner(s) for s in range(groups) if s != middle]:
            part_of = res.at[here, pl.ds(pl.multiple_of(peer * owned, owned), owned), :]
            remote(part_of, there, send_out, recv_out, {"mode": peer}).start()
        pltpu.make_async_copy(res.at[here, mine, :], there, recv_out).start()
        return carry

    lax.fori_loop(0, nrows, step, 0)

    pl.when(closes)(kap_after.wait_send)
    pl.when(opens)(kap_before.wait_send)
    for wanted, copy in edges:
        pl.when(wanted)(copy.wait_send)
    pl.when(gives_after)(fwd_after.wait_send)
    pl.when(gives_before)(fwd_before.wait_send)
    arrived(gath.at[pl.ds(0, nrows), others, :], send_in)
    arrived(res.at[:, others, :], send_out)
    arrived(out, recv_out)


def exchange(field, kappa, mass, kl, tp, fp, cap, lat):
    groups, parts = lax.axis_size("mode"), lax.axis_size("mesh")
    owned, total_rows, width = field.shape
    nrows, modes = mass.shape[0], tp.shape[1]
    terms = kl.shape[0]
    vmem = pl.BlockSpec(memory_space=pltpu.VMEM)
    hbm = pl.BlockSpec(memory_space=pl.ANY)
    work = modes * nrows * width
    dma = pltpu.SemaphoreType.DMA
    return pl.pallas_call(
        functools.partial(kernel, groups, parts),
        out_shape=jax.ShapeDtypeStruct((total_rows, owned, width), jnp.bfloat16),
        in_specs=[hbm, vmem, vmem, hbm, hbm, hbm, vmem, vmem],
        out_specs=hbm,
        scratch_shapes=[
            pltpu.VMEM((2, owned, LOAD, width), jnp.float32),
            pltpu.VMEM((total_rows, owned, width), jnp.bfloat16),
            pltpu.VMEM((nrows + 2, modes, width), jnp.bfloat16),
            pltpu.VMEM((nrows, modes, width), jnp.bfloat16),
            pltpu.VMEM((terms, modes, width), jnp.bfloat16),
            pltpu.VMEM((terms * 4, nrows, width), jnp.float32),
            pltpu.VMEM((2,) + kappa.shape, jnp.bfloat16),
            pltpu.VMEM(kl.shape, kl.dtype),
            pltpu.VMEM(tp.shape, tp.dtype),
            pltpu.VMEM(fp.shape, fp.dtype),
            dma((2,)),
            dma((nrows // LOAD,)),
            dma((2,)),
            dma((2,)),
            dma,
            dma,
            dma((4,)),
            dma((2,)),
            dma((2,)),
            dma,
            dma((3,)),
        ],
        compiler_params=pltpu.CompilerParams(
            collective_id=0, has_side_effects=True, vmem_limit_bytes=48 * 1024 * 1024
        ),
        cost_estimate=pl.CostEstimate(
            flops=2 * work * (terms * modes + 2 * tp.shape[0]),
            bytes_accessed=6 * work,
            transcendentals=nrows * width * tp.shape[0],
        ),
    )(field, kappa, mass, kl, tp, fp, cap[:, None], lat[:, None])


def exchange_small(ext, coef, mass, kl, tp, fp, cap, lat):
    groups = lax.axis_size("mode")
    owned, width = ext.shape[1:]
    nrows, modes = mass.shape[0], tp.shape[1]
    terms = coef.shape[1] // 4
    parts = jnp.stack([ext[d * nrows : d * nrows + nrows + 2] for d in range(groups)], 0)
    moved = lax.all_to_all(parts, "mode", split_axis=0, concat_axis=0, tiled=True)
    rows = jnp.moveaxis(moved, 0, 1).reshape(nrows + 2, modes, width)
    own = rows[1:-1]
    v = jnp.pad(rows.astype(jnp.float32), ((0, 0), (0, 0), (1, 1)))
    centre = v[1:-1, :, 1:-1]
    others = (v[:-2, :, 1:-1], v[2:, :, 1:-1], v[1:-1, :, :-2], v[1:-1, :, 2:])
    images = [
        sum(coef[:, 4 * k + d, None, :] * (centre - others[d]) for d in range(4)).astype(jnp.bfloat16)
        for k in range(terms)
    ]
    images = jnp.concatenate(images, 1)
    mixed = jnp.einsum("ij,rjx->rix", kl, images, preferred_element_type=jnp.float32)
    temps = jnp.einsum("qi,rix->rqx", tp, own, preferred_element_type=jnp.float32)
    heat = (cap[:, None] * temps + lat[:, None] * jax.nn.sigmoid(2.0 * temps)).astype(jnp.bfloat16)
    enthalpy = jnp.einsum("iq,rqx->rix", fp, heat, preferred_element_type=jnp.float32)
    result = (mass[:, None, :] * enthalpy + mixed).astype(jnp.bfloat16)
    result = result.reshape(nrows, groups, owned, width)
    back = lax.all_to_all(result, "mode", split_axis=1, concat_axis=0, tiled=True)
    return back.reshape(nrows * groups, owned, width)


def body(field, kappa, mass, kl_modes, to_points, from_points, capacity, latent):
    nrows, owned = mass.shape[0], field.shape[0]
    fits = owned % 16 == 0 and nrows % 16 == 0 and field.shape[2] % TILE == 0
    if fits:
        out = exchange(field, kappa, mass, kl_modes, to_points, from_points, capacity, latent)
        return jnp.transpose(out, (1, 0, 2))
    coarse = jnp.transpose(field.astype(jnp.bfloat16), (1, 0, 2))
    up, down = halo(coarse, "mesh")
    ext = jnp.concatenate([up, coarse, down], 0)
    coef = weights_of(kappa)
    terms, modes = kl_modes.shape[:2]
    kl = jnp.transpose(kl_modes, (1, 0, 2)).reshape(modes, terms * modes)
    out = exchange_small(ext, coef, mass, kl, to_points, from_points, capacity, latent)
    return jnp.transpose(out, (1, 0, 2))


def solution(mesh):
    in_specs = (
        P("mode", "mesh", None),
        P(None, ("mesh", "mode"), None),
        P(("mesh", "mode"), None),
        P(),
        P(),
        P(),
        P(),
        P(),
    )
    out_specs = P("mode", "mesh", None)
    return jax.shard_map(body, mesh=mesh, in_specs=in_specs, out_specs=out_specs, check_vma=False)
```
